128 devices in a mesh: ep: 16 (over z, x), etp: 8 (over y, core).
Axes of the slice: x: 4, y: 4, z: 4, core: 2. Of those that a mesh axis runs over, the one named last changes fastest.
Arguments:
- tokens: bfloat16 [2048, 3072], P('ep', 'etp'), may hold values from -6 to 6
- grad_out: bfloat16 [2048, 3072], P('ep', 'etp'), may hold values from -6 to 6
- probs: float32 [2048, 4], P('ep'), may hold values from 0.1 to 1
- expert_ids: int32 [2048, 4], P('ep'), may hold values from 0 to 15, all different within a row; in each aligned block of 128 rows (0 to 127, 128 to 255, ...) at most 48 rows name the same one
- w_gate: bfloat16 [16, 3072, 5376], P('ep', None, 'etp'), may hold values from -0.109375 to 0.109375
- w_up: bfloat16 [16, 3072, 5376], P('ep', None, 'etp'), may hold values from -0.109375 to 0.109375
- w_down: bfloat16 [16, 5376, 3072], P('ep', 'etp'), may hold values from -0.078125 to 0.078125
Outputs:
- grad_tokens: bfloat16 [2048, 3072], P('ep', 'etp')
- grad_gate: bfloat16 [16, 3072, 5376], P('ep', None, 'etp')
- grad_up: bfloat16 [16, 3072, 5376], P('ep', None, 'etp')
- grad_down: bfloat16 [16, 5376, 3072], P('ep', 'etp')
The draws below stay inside these ranges and needn't reach their ends.
Inputs may be any that keep to these rules, and one draw needn't show every extreme that they name: `expert_ids`: each row names 4 different experts. In the rows of one index of ep (aligned blocks of 128 rows) no expert is named by more than 48 rows, a bound that some block reaches.
All inputs are finite; a program needn't handle non-finite values.
Results may differ from the reference program's by a relative error of at most 0.02.
Values may be sent and summed in bfloat16 or wider, within the bound.
A program may use at most 128 MiB of HBM per device.

```python
import math
import jax
import jax.numpy as jnp
import numpy as np
from jax import lax

D = 3072
FF = 5376
TOPK = 4
TOK_DEV = 128
EXPERTS = 16
CAP = 48
ROWS = 768
FF_DEV = 672
TOKENS = 2048


def block_scale(key, shape, pieces, low, largest):
    gain = 1.0
    for axis_at, parts in pieces:
        heights = jax.random.uniform(jax.random.fold_in(jax.random.fold_in(key, 6), axis_at), (parts,), jnp.float32, low / len(pieces), largest / len(pieces))
        gain = gain * jnp.repeat(jnp.exp(heights), shape[axis_at] // parts).reshape((-1,) + (1,) * (len(shape) - 1 - axis_at))
    return gain


def shared_out(own_key, own, number, rows, count, top, reach, lean):
    order = jax.random.permutation(own_key, count)
    crowded, common = portions_of(count, rows * top, reach, lean, True), portions_of(count, rows * top, reach, lean, False)
    places = jnp.arange(count)

    def named(lengths, offset_by):
        used = int((lengths > 0).sum())
        fixed = max(1, used // 4)
        shifted = fixed + (places - fixed + offset_by * (used - fixed)) % max(1, count - fixed)
        return jnp.zeros((count,), jnp.int32).at[order[jnp.where(places < fixed, places, shifted)]].set(jnp.asarray(lengths, jnp.int32))

    lengths = jnp.where(number % 4 == 0, named(crowded, number // 4), named(common, number - number // 4 - 1))
    mixed = jax.random.permutation(jax.random.fold_in(own, 3), count)
    donor, sink = mixed[0:count // 2 * 2:2], mixed[1:count // 2 * 2:2]
    margin = jnp.minimum(lengths[donor] - 1, reach - lengths[sink]) // 2
    margin = jnp.where((donor == order[0]) | (sink == order[0]) | (lengths[sink] == 0), 0, jnp.maximum(margin, 0))
    shifted = jax.random.randint(jax.random.fold_in(own, 4), (count // 2,), 0, 1 << 20) % (margin + 1)
    lengths = lengths.at[donor].add(-shifted).at[sink].add(shifted)
    members = jnp.searchsorted(jnp.cumsum(lengths), jnp.arange(rows * top), side="right").astype(jnp.int32)
    table = members.reshape(top, rows).T
    table = table[jax.random.permutation(jax.random.fold_in(own, 1), rows)]
    offset_by = jax.random.randint(jax.random.fold_in(own, 2), (rows, 1), 0, top)
    return jnp.take_along_axis(table, (jnp.arange(top)[None, :] + offset_by) % top, axis=1)


def portions_of(amount, total, reach, lean, full):
    portions = [(1 << 20) // math.isqrt(rank ** lean) + 1 for rank in range(1, amount + 1)]
    largest = reach if full else min(reach, max(-(-total // amount), total * portions[0] // sum(portions)))
    least = 1 if total - largest >= amount - 1 else 0
    holding, spare = [largest] + [least] * (amount - 1), total - largest - least * (amount - 1)
    while spare > 0:
        free = [i for i in range(1, amount) if holding[i] < largest] or [i for i in range(1, amount) if holding[i] < reach]
        whole, left = sum([portions[i] for i in free]), spare
        for i in free:
            extra = min(reach - holding[i], max(1, left * portions[i] // whole), spare)
            holding[i] = holding[i] + extra
            spare = spare - extra
    return np.array(holding)


def scatter_about(stream_key, extent, spread, bound, pieces=(), held_as=jnp.bfloat16):
    array = spread * jax.random.normal(stream_key, extent, jnp.float32)
    if pieces:
        array = array * block_scale(stream_key, extent, pieces, -0.22, 0.18)
    return jnp.clip(array, -bound, bound).astype(held_as)


def setup_inputs(seed: int = 0) -> dict:
    key_list = jax.random.split(jax.random.key(seed), 8)
    tokens = scatter_about(key_list[0], (TOKENS, D), 1.0, 6.0, ((0, 16), (1, 8)))
    grad_out = scatter_about(key_list[1], (TOKENS, D), 1.0, 6.0, ((0, 16), (1, 8)))
    probs = jnp.clip(0.1 + 0.9 * jax.random.uniform(key_list[2], (TOKENS, TOPK), jnp.float32) ** block_scale(key_list[2], (TOKENS, TOPK), ((0, 16),), -0.2, 0.2), 0.1, 1.0)
    expert_ids_keys = jax.random.split(jax.random.fold_in(key_list[3], 1), TOKENS // TOK_DEV)
    expert_ids_turns = jax.random.permutation(jax.random.fold_in(key_list[3], 3), TOKENS // TOK_DEV)
    expert_ids = jax.vmap(lambda own, number: shared_out(jax.random.fold_in(key_list[3], 2), own, number, TOK_DEV, EXPERTS, TOPK, CAP, 2))(expert_ids_keys, expert_ids_turns).reshape((TOKENS, TOPK))
    w_gate = scatter_about(key_list[4], (EXPERTS, D, FF), D ** -0.5, 0.109375, ((0, 16), (2, 8)))
    w_up = scatter_about(key_list[5], (EXPERTS, D, FF), D ** -0.5, 0.109375, ((0, 16), (2, 8)))
    w_down = scatter_about(key_list[6], (EXPERTS, FF, D), FF ** -0.5, 0.078125, ((0, 16), (1, 8)))
    return {"tokens": tokens, "grad_out": grad_out, "probs": probs, "expert_ids": expert_ids, "w_gate": w_gate, "w_up": w_up, "w_down": w_down}


def slot_index(block_ids, capacity, expert_count):
    flat_ids = block_ids.reshape(-1).astype(jnp.int32)
    onehot = (flat_ids[:, None] == jnp.arange(expert_count, dtype=jnp.int32)[None, :]).astype(jnp.int32)
    earlier = jnp.cumsum(onehot, axis=0) - onehot
    position = jnp.sum(earlier * onehot, axis=1)
    return (flat_ids * capacity + position).astype(jnp.int32)


def swiglu_back(gate_pre, up_pre, grad_hidden):
    sigmoid_gate = jax.nn.sigmoid(gate_pre)
    silu_gate = gate_pre * sigmoid_gate
    hidden = silu_gate * up_pre
    grad_pre_gate = grad_hidden * up_pre * sigmoid_gate * (1.0 + gate_pre * (1.0 - sigmoid_gate))
    grad_pre_up = grad_hidden * silu_gate
    return hidden, grad_pre_gate, grad_pre_up


def reference(tokens, grad_out, probs, expert_ids, w_gate, w_up, w_down):
    block_ids = expert_ids.reshape(EXPERTS, TOK_DEV, TOPK)
    slot_ids = jax.vmap(lambda ids: slot_index(ids, CAP, EXPERTS))(block_ids)
    scaled = (probs[:, :, None] * grad_out.astype(jnp.float32)[:, None, :]).astype(jnp.bfloat16)
    copies_in = jnp.repeat(tokens, TOPK, axis=0).reshape(EXPERTS, TOK_DEV * TOPK, D)
    copies_grad = scaled.reshape(EXPERTS, TOK_DEV * TOPK, D)

    def place_rows(slot_row, copies):
        return jnp.zeros((EXPERTS * CAP, D), copies.dtype).at[slot_row].set(copies)

    def arrange(copies):
        placed = jax.vmap(place_rows)(slot_ids, copies)
        placed = placed.reshape(EXPERTS, EXPERTS, CAP, D).transpose(1, 0, 2, 3)
        return placed.reshape(EXPERTS, ROWS, D)

    expert_in = arrange(copies_in)
    expert_grad = arrange(copies_grad)

    def one_expert(operands):
        rows_in, rows_grad, gate_w, up_w, down_w = operands
        gate_pre = jnp.dot(rows_in, gate_w, preferred_element_type=jnp.float32)
        up_pre = jnp.dot(rows_in, up_w, preferred_element_type=jnp.float32)
        grad_hidden = jnp.dot(rows_grad, down_w.T, preferred_element_type=jnp.float32)
        hidden, grad_pre_gate, grad_pre_up = swiglu_back(gate_pre, up_pre, grad_hidden)
        hidden = hidden.astype(jnp.bfloat16)
        grad_pre_gate = grad_pre_gate.astype(jnp.bfloat16)
        grad_pre_up = grad_pre_up.astype(jnp.bfloat16)
        down_grad = jnp.dot(hidden.T, rows_grad, preferred_element_type=jnp.float32).astype(jnp.bfloat16)
        gate_grad = jnp.dot(rows_in.T, grad_pre_gate, preferred_element_type=jnp.float32).astype(jnp.bfloat16)
        up_grad = jnp.dot(rows_in.T, grad_pre_up, preferred_element_type=jnp.float32).astype(jnp.bfloat16)
        ranges = FF // FF_DEV
        gate_parts = grad_pre_gate.astype(jnp.float32).reshape(ROWS, ranges, FF_DEV)
        up_parts = grad_pre_up.astype(jnp.float32).reshape(ROWS, ranges, FF_DEV)
        gate_rows = gate_w.astype(jnp.float32).reshape(D, ranges, FF_DEV)
        up_rows = up_w.astype(jnp.float32).reshape(D, ranges, FF_DEV)
        partial_value = jnp.einsum("rnf,dnf->rnd", gate_parts, gate_rows) + jnp.einsum("rnf,dnf->rnd", up_parts, up_rows)
        summed = jnp.sum(partial_value.astype(jnp.bfloat16).astype(jnp.float32), axis=1)
        return gate_grad, up_grad, down_grad, summed

    grad_gate, grad_up, grad_down, summed = lax.map(one_expert, (expert_in, expert_grad, w_gate, w_up, w_down))
    back = summed.reshape(EXPERTS, EXPERTS, CAP, D).transpose(1, 0, 2, 3).reshape(EXPERTS, EXPERTS * CAP, D)
    picked = jax.vmap(lambda table, slot_row: table[slot_row])(back, slot_ids)
    grad_tokens = jnp.sum(picked.reshape(TOKENS, TOPK, D), axis=1).astype(jnp.bfloat16)
    return grad_tokens, grad_gate, grad_up, grad_down
```

```python
import functools
import jax
import jax.numpy as jnp
from jax import lax
from jax.experimental import pallas as pl
from jax.experimental.pallas import tpu as pltpu
from jax.sharding import PartitionSpec as P

BF = jnp.bfloat16
F32 = jnp.float32
CAP = 48
SLOTS = 16
ROWS = CAP * SLOTS
GROUP = 4
GROWS = GROUP * CAP
CHUNKS = ((0, 2), (2, 4))
MESH = pl.DeviceIdType.MESH


def nt(a, b):
    return lax.dot_general(a, b, (((1,), (1,)), ((), ())), preferred_element_type=F32)


def tn(a, b):
    return lax.dot_general(a, b, (((0,), (0,)), ((), ())), preferred_element_type=F32)


def nn(a, b):
    return jnp.dot(a, b, preferred_element_type=F32)


def expert_kernel(
    tokens, gout, ids, probs, wg_h, wu_h, wd_h,
    gt_out, gg_h, gu_h, gd_h,
    xg, snd, raw, wg, wu, wd, place, pw,
    hid, gpg, gpu, acc_g, acc_u, acc_h,
    part, from_sib, from_y, snd_back, back, tail_snd, tail_rcv, stage_g, stage_d,
    sem_w, sem_raw, sem_self, sem_send, sem_recv, sem_fsend, sem_frecv,
    sem_psend, sem_precv, sem_ysend, sem_yrecv, sem_bself, sem_bsend, sem_brecv, sem_tail, sem_out,
):
    ep = lax.axis_index("ep")
    t = lax.axis_index("etp")
    z, x = ep // 4, ep % 4
    y, core = t // 2, t % 2
    width = tokens.shape[1]
    t_up, t_down, t_far = (t + 2) % 8, (t + 6) % 8, (t + 4) % 8
    t_sib = t + 1 - 2 * core

    def target(j):
        i = j % 4
        return ((z + i) % 4) * 4 + (x + i + j // 4) % 4

    def source(j):
        i = j % 4
        return ((z + 4 - i) % 4) * 4 + (x + 8 - i - j // 4) % 4

    def cols(f):
        return pl.ds(pl.multiple_of(f * width, 128), width)

    def slot(j):
        return pl.ds(pl.multiple_of(j * CAP, 16), CAP)

    def remote(src, dst, ss, rs, e, f):
        return pltpu.make_async_remote_copy(
            src_ref=src, dst_ref=dst, send_sem=ss, recv_sem=rs,
            device_id={"ep": e, "etp": f}, device_id_type=MESH,
        )

    w_copies = [
        pltpu.make_async_copy(h.at[0], v, sem_w.at[i])
        for i, (h, v) in enumerate(((wg_h, wg), (wu_h, wu), (wd_h, wd)))
    ]
    for copy in w_copies:
        copy.start()

    barrier = pltpu.get_barrier_semaphore()

    @pl.loop(1, SLOTS)
    def _(j):
        pl.semaphore_signal(barrier, inc=1, device_id={"ep": target(j), "etp": t}, device_id_type=MESH)

    for f in (t_up, t_down, t_far, t_sib):
        pl.semaphore_signal(barrier, inc=1, device_id={"ep": ep, "etp": f}, device_id_type=MESH)

    lane = lax.broadcasted_iota(jnp.int32, (128, 128), 1)
    row = lax.broadcasted_iota(jnp.int32, (128, 128), 0)
    li = lane & 3
    expert = ((z + li) & 3) * 4 + ((x + li + (lane >> 2)) & 3)
    expert = jnp.where(lane < SLOTS, expert, -1)
    hit = jnp.zeros((128, 128), F32)
    weight = jnp.zeros((128, 128), F32)
    for k in range(ids.shape[1]):
        same = ids[:, k : k + 1] == expert
        hit = hit + jnp.where(same, 1.0, 0.0)
        weight = weight + jnp.where(same, probs[:, k : k + 1], 0.0)
    hit = hit.T[:SLOTS]
    weight = weight.T[:SLOTS]
    earlier = jnp.where(row < lane, 1.0, 0.0).astype(BF)
    pos = nn(hit.astype(BF), earlier)
    rank = lax.broadcasted_iota(jnp.int32, (CAP, 128), 0).astype(F32)
    for j in range(SLOTS):
        one = jnp.where(pos[j : j + 1] == rank, hit[j : j + 1], 0.0)
        place[j * CAP : (j + 1) * CAP, :] = one.astype(BF)
        pw[j * CAP : (j + 1) * CAP, :] = jnp.broadcast_to(
            jnp.sum(one * weight[j : j + 1], axis=1, keepdims=True), (CAP, 128)
        )

    pl.semaphore_wait(barrier, SLOTS - 1 + 4)

    raw_copies = [
        remote(src, raw.at[i], sem_raw.at[0, i], sem_raw.at[1, i], ep, t_far)
        for i, src in enumerate((tokens, gout))
    ]
    for copy in raw_copies:
        copy.start()

    def fill(b, g, tok, grad):
        rows = pl.ds(g * GROWS, GROWS)
        one = place[rows, :]
        snd[b, 0, rows, :] = nn(one, tok).astype(BF)
        snd[b, 1, rows, :] = (nn(one, grad) * pw[rows, 0:1]).astype(BF)

    def own_copy(b):
        f = (t, t_far)[b]
        return pltpu.make_async_copy(
            snd.at[b, :, pl.ds(0, CAP), :], xg.at[:, pl.ds(0, CAP), cols(f)], sem_self.at[b]
        )

    def out_copy(b, j, e):
        f = (t, t_far)[b]
        return remote(
            snd.at[b, :, slot(j), :], xg.at[:, slot(j), cols(f)],
            sem_send.at[b, j], sem_recv.at[b, j], e, t,
        )

    def send(b, g):
        if g == 0:
            own_copy(b).start()

        @pl.loop(max(1, g * GROUP), (g + 1) * GROUP)
        def _(j):
            out_copy(b, j, target(j)).start()

    def fwd_copy(kind, g):
        rows = pl.ds(g * GROWS, GROWS)
        f = (t, t, t, t_far, t_down, t_up)[kind]
        to = (t_up, t_down, t_sib, t_sib, t_sib, t_sib)[kind]
        ref = xg.at[:, rows, cols(f)]
        return remote(ref, ref, sem_fsend.at[kind, g], sem_frecv.at[kind, g], ep, to)

    def arrived(kind, g):
        rows = pl.ds(g * GROWS, GROWS)
        f = (t_down, t_up, t_sib, (t_sib + 4) % 8, (t_sib + 6) % 8, (t_sib + 2) % 8)[kind]
        ref = xg.at[:, rows, cols(f)]
        return remote(ref, ref, sem_fsend.at[kind, g], sem_frecv.at[kind, g], ep, t_sib)

    def got(b, g):
        if g == 0:
            own_copy(b).wait()

        @pl.loop(max(1, g * GROUP), (g + 1) * GROUP)
        def _(j):
            out_copy(b, j, source(j)).wait_recv()

    def fwd_a(g):
        got(0, g)
        for kind in (0, 1, 2):
            fwd_copy(kind, g).start()

    def fwd_b(g):
        got(1, g)
        fwd_copy(3, g).start()

    def fwd_y(g):
        for kind in (0, 1):
            arrived(kind, g).wait_recv()
            fwd_copy(4 + kind, g).start()

    def whole(g):
        for kind in (2, 3, 4, 5):
            arrived(kind, g).wait_recv()

    for g in range(4):
        fill(0, g, tokens[...], gout[...])
        send(0, g)
        if g == 1:
            for copy in raw_copies:
                copy.wait_recv()
        if g >= 1:
            fill(1, g - 1, raw[0], raw[1])
            send(1, g - 1)
    fill(1, 3, raw[0], raw[1])
    send(1, 3)

    def tiles(n, body, services=None):
        services = services or {}

        @pl.loop(0, n)
        def _(k):
            body(k)
            for at, calls in services.items():
                @pl.when(k == at)
                def _():
                    for call in calls:
                        call()

    def forward(c, services=None):
        g0, g1 = CHUNKS[c]
        n = (g1 - g0) * GROWS
        rows = pl.ds(g0 * GROWS, n)
        top = pl.ds(0, n)
        tile = 512

        def body(k):
            ks = pl.ds(pl.multiple_of(k * tile, tile), tile)
            xk = xg[0, rows, ks]
            gk = xg[1, rows, ks]
            g = nn(xk, wg[ks, :])
            u = nn(xk, wu[ks, :])
            h = nt(gk, wd[:, ks])

            @pl.when(k == 0)
            def _():
                acc_g[top, :] = g
                acc_u[top, :] = u
                acc_h[top, :] = h

            @pl.when(k > 0)
            def _():
                acc_g[top, :] += g
                acc_u[top, :] += u
                acc_h[top, :] += h

        tiles(xg.shape[2] // tile, body, services)
        piece = 96

        @pl.loop(0, n // piece)
        def _(i):
            rs = pl.ds(pl.multiple_of(i * piece, piece), piece)
            rd = pl.ds(pl.multiple_of(g0 * GROWS + i * piece, 16), piece)
            g = acc_g[rs, :]
            u = acc_u[rs, :]
            h = acc_h[rs, :]
            s = jax.nn.sigmoid(g)
            sg = g * s
            hid[rd, :] = (sg * u).astype(BF)
            gpg[rd, :] = (h * u * s * (1.0 + g * (1.0 - s))).astype(BF)
            gpu[rd, :] = (h * sg).astype(BF)

    steps = (1, 3, 2, 0)

    def chunk_rows(c):
        g0, g1 = CHUNKS[c]
        return pl.ds(g0 * GROWS, (g1 - g0) * GROWS)

    def sib_copy(c, i):
        rows = chunk_rows(c)
        return remote(
            part.at[i, 1 - core, rows, :], from_sib.at[i, rows, :],
            sem_psend.at[c, i], sem_precv.at[c, i], ep, t_sib,
        )

    def y_copy(c, i):
        rows = chunk_rows(c)
        return remote(
            part.at[i, core, rows, :], from_y.at[i, rows, :],
            sem_ysend.at[c, i], sem_yrecv.at[c, i], ep, (t_up, t_down)[i],
        )

    def quarter(c, i):
        rows = chunk_rows(c)
        q = (y + steps[i]) % 4
        ws = pl.ds(pl.multiple_of(q * 2 * width, 128), 2 * width)
        p = nt(gpg[rows, :], wg[ws, :]) + nt(gpu[rows, :], wu[ws, :])
        part[i, 0, rows, :] = p[:, :width].astype(BF)
        part[i, 1, rows, :] = p[:, width:].astype(BF)
        sib_copy(c, i).start()

    def pair(c, i):
        rows = chunk_rows(c)
        sib_copy(c, i).wait_recv()
        return part[i, core, rows, :].astype(F32) + from_sib[i, rows, :].astype(F32)

    def pair_y(c, i):
        part[i, core, chunk_rows(c), :] = pair(c, i).astype(BF)
        y_copy(c, i).start()

    def back_copy(b, j, e):
        return remote(
            snd_back.at[b, slot(j), :], back.at[b, slot(j), :],
            sem_bsend.at[b, j], sem_brecv.at[b, j], e, t,
        )

    def own_back(b):
        return pltpu.make_async_copy(
            snd_back.at[b, pl.ds(0, CAP), :], back.at[b, pl.ds(0, CAP), :], sem_bself.at[b]
        )

    def send_back(c, b):
        g0, g1 = CHUNKS[c]
        if g0 == 0:
            own_back(b).start()

        @pl.loop(max(1, g0 * GROUP), g1 * GROUP)
        def _(j):
            back_copy(b, j, source(j)).start()

    def pair_far(c):
        snd_back[1, chunk_rows(c), :] = pair(c, 2).astype(BF)
        send_back(c, 1)

    def pair_own(c):
        rows = chunk_rows(c)
        mine = pair(c, 3)
        for i in (0, 1):
            y_copy(c, i).wait_recv()
            mine = mine + from_y[i, rows, :].astype(F32)
        snd_back[0, rows, :] = mine.astype(BF)
        send_back(c, 0)

    tail = remote(tail_snd, tail_rcv, sem_tail.at[0], sem_tail.at[1], ep, t_far)

    def got_back(b):
        own_back(b).wait()

        @pl.loop(1, SLOTS)
        def _(j):
            back_copy(b, j, target(j)).wait_recv()

    def combine_far():
        got_back(1)
        tail_snd[...] = tn(place[...], back[1]).astype(BF)
        tail.start()

    def combine_own():
        got_back(0)
        mine = tn(place[...], back[0])
        tail.wait_recv()
        gt_out[...] = (mine + tail_rcv[...].astype(F32)).astype(BF)

    wt = 512

    def down_copy(k):
        ks = pl.ds(pl.multiple_of(k * wt, wt), wt)
        return pltpu.make_async_copy(stage_d.at[k % 2], gd_h.at[0, :, ks], sem_out.at[0, k % 2])

    def gate_copy(k, i):
        ks = pl.ds(pl.multiple_of(k * wt, wt), wt)
        return pltpu.make_async_copy(stage_g.at[i, k % 2], (gg_h, gu_h)[i].at[0, ks, :], sem_out.at[1 + i, k % 2])

    def down_tile(k):
        ks = pl.ds(pl.multiple_of(k * wt, wt), wt)

        @pl.when(k >= 2)
        def _():
            down_copy(k - 2).wait()

        stage_d[k % 2] = tn(hid[...], xg[1, :, ks]).astype(BF)
        down_copy(k).start()

    def gate_tile(k):
        ks = pl.ds(pl.multiple_of(k * wt, wt), wt)
        for i in (0, 1):
            @pl.when(k >= 2)
            def _():
                gate_copy(k - 2, i).wait()

            stage_g[i, k % 2] = tn(xg[0, :, ks], (gpg, gpu)[i][...]).astype(BF)
            gate_copy(k, i).start()

    nw = xg.shape[2] // wt

    fwd_a(0)
    fwd_a(1)
    fwd_b(0)
    fwd_y(0)
    fwd_b(1)
    fwd_a(2)
    fwd_y(1)
    for copy in w_copies:
        copy.wait()
    whole(0)
    whole(1)
    forward(0, {
        0: [lambda: fwd_b(2)], 1: [lambda: fwd_a(3)], 2: [lambda: fwd_y(2)],
        3: [lambda: fwd_b(3)], 5: [lambda: fwd_y(3)],
    })
    quarter(0, 0)
    quarter(0, 1)
    pair_y(0, 0)
    quarter(0, 2)
    pair_y(0, 1)
    quarter(0, 3)
    pair_far(0)
    whole(2)
    whole(3)
    forward(1, {1: [lambda: pair_own(0)]})
    quarter(1, 0)
    quarter(1, 1)
    pair_y(1, 0)
    quarter(1, 2)
    pair_y(1, 1)
    quarter(1, 3)
    pair_far(1)
    tiles(nw, down_tile, {2: [lambda: pair_own(1)]})
    tiles(nw, gate_tile, {2: [combine_far], 4: [combine_own]})

    for k in (nw - 2, nw - 1):
        down_copy(k).wait()
        for i in (0, 1):
            gate_copy(k, i).wait()
    for copy in raw_copies:
        copy.wait_send()
    tail.wait_send()
    for b in (0, 1):
        @pl.loop(1, SLOTS)
        def _(j):
            out_copy(b, j, target(j)).wait_send()
            back_copy(b, j, source(j)).wait_send()

    for g in range(4):
        for kind in range(6):
            fwd_copy(kind, g).wait_send()
    for c in range(len(CHUNKS)):
        for i in range(4):
            sib_copy(c, i).wait_send()
        for i in range(2):
            y_copy(c, i).wait_send()


def local(tokens, grad_out, probs, expert_ids, w_gate, w_up, w_down):
    toks, width = tokens.shape
    _, d, ff = w_gate.shape
    vmem = pl.BlockSpec(memory_space=pltpu.VMEM)
    hbm = pl.BlockSpec(memory_space=pl.ANY)
    dma = pltpu.SemaphoreType.DMA
    n = max(b - a for a, b in CHUNKS) * GROWS
    nc = len(CHUNKS)
    gt, gg, gu, gd = pl.pallas_call(
        expert_kernel,
        out_shape=[
            jax.ShapeDtypeStruct((toks, width), BF),
            jax.ShapeDtypeStruct(w_gate.shape, BF),
            jax.ShapeDtypeStruct(w_up.shape, BF),
            jax.ShapeDtypeStruct(w_down.shape, BF),
        ],
        in_specs=[vmem] * 4 + [hbm] * 3,
        out_specs=[vmem] + [hbm] * 3,
        scratch_shapes=[
            pltpu.VMEM((2, ROWS, d), BF),
            pltpu.VMEM((2, 2, ROWS, width), BF),
            pltpu.VMEM((2, toks, width), BF),
            pltpu.VMEM((d, ff), BF),
            pltpu.VMEM((d, ff), BF),
            pltpu.VMEM((ff, d), BF),
            pltpu.VMEM((ROWS, toks), BF),
            pltpu.VMEM((ROWS, 128), F32),
            pltpu.VMEM((ROWS, ff), BF),
            pltpu.VMEM((ROWS, ff), BF),
            pltpu.VMEM((ROWS, ff), BF),
            pltpu.VMEM((n, ff), F32),
            pltpu.VMEM((n, ff), F32),
            pltpu.VMEM((n, ff), F32),
            pltpu.VMEM((4, 2, ROWS, width), BF),
            pltpu.VMEM((4, ROWS, width), BF),
            pltpu.VMEM((2, ROWS, width), BF),
            pltpu.VMEM((2, ROWS, width), BF),
            pltpu.VMEM((2, ROWS, width), BF),
            pltpu.VMEM((toks, width), BF),
            pltpu.VMEM((toks, width), BF),
            pltpu.VMEM((2, 2, 512, ff), BF),
            pltpu.VMEM((2, ff, 512), BF),
            dma((3,)),
            dma((2, 2)),
            dma((2,)),
            dma((2, SLOTS)),
            dma((2, SLOTS)),
            dma((6, 4)),
            dma((6, 4)),
            dma((nc, 4)),
            dma((nc, 4)),
            dma((nc, 2)),
            dma((nc, 2)),
            dma((2,)),
            dma((2, SLOTS)),
            dma((2, SLOTS)),
            dma((2,)),
            dma((3, 2)),
        ],
        compiler_params=pltpu.CompilerParams(
            collective_id=0, has_side_effects=True, vmem_limit_bytes=60 * 2**20
        ),
    )(tokens, grad_out, expert_ids, probs, w_gate, w_up, w_down)
    return gt, gg, gu, gd


def solution(mesh):
    return jax.shard_map(
        local,
        mesh=mesh,
        in_specs=(
            P("ep", "etp"),
            P("ep", "etp"),
            P("ep", None),
            P("ep", None),
            P("ep", None, "etp"),
            P("ep", None, "etp"),
            P("ep", "etp", None),
        ),
        out_specs=(
            P("ep", "etp"),
            P("ep", None, "etp"),
            P("ep", None, "etp"),
            P("ep", "etp", None),
        ),
        check_vma=False,
    )
```

```python
import functools
import jax
import jax.numpy as jnp
from jax import lax
from jax.experimental import pallas as pl
from jax.experimental.pallas import tpu as pltpu
from jax.sharding import PartitionSpec as P

BF = jnp.bfloat16
F32 = jnp.float32
CAP = 48
SLOTS = 16
ROWS = CAP * SLOTS
UNIT = 2
UROWS = UNIT * CAP
UNITS = SLOTS // UNIT
CHUNK = 256
CHUNKS = ROWS // CHUNK
BACK = (0, 5, 10, SLOTS)
MESH = pl.DeviceIdType.MESH


def nt(a, b):
    return lax.dot_general(a, b, (((1,), (1,)), ((), ())), preferred_element_type=F32)


def tn(a, b):
    return lax.dot_general(a, b, (((0,), (0,)), ((), ())), preferred_element_type=F32)


def nn(a, b):
    return jnp.dot(a, b, preferred_element_type=F32)


def expert_kernel(
    tokens, gout, ids_h, probs_h, wg_h, wu_h, wd_h,
    gt_out, gg_h, gu_h, gd_h,
    xg, snd, raw, tok_v, gout_v, ids, probs, wg, wu, wd, place, pw,
    hid, gpg, gpu, acc_g, acc_u, acc_h,
    part, from_sib, from_y, snd_back, back, tail_snd, tail_rcv,
    sem_in, sem_w, sem_raw, sem_self, sem_send, sem_recv, sem_fsend, sem_yget, sem_sget,
    sem_psend, sem_precv, sem_ysend, sem_yrecv, sem_bself, sem_bsend, sem_brecv, sem_tail,
):
    ep = lax.axis_index("ep")
    t = lax.axis_index("etp")
    z, x = ep // 4, ep % 4
    y, core = t // 2, t % 2
    width = tokens.shape[1]
    t_up, t_down, t_far = (t + 2) % 8, (t + 6) % 8, (t + 4) % 8
    t_sib = t + 1 - 2 * core

    def target(j):
        i = j % 4
        return ((z + i) % 4) * 4 + (x + i + j // 4) % 4

    def source(j):
        i = j % 4
        return ((z + 4 - i) % 4) * 4 + (x + 8 - i - j // 4) % 4

    def cols(f):
        return pl.ds(pl.multiple_of(f * width, 128), width)

    def slot(j):
        return pl.ds(pl.multiple_of(j * CAP, 16), CAP)

    def remote(src, dst, ss, rs, e, f):
        return pltpu.make_async_remote_copy(
            src_ref=src, dst_ref=dst, send_sem=ss, recv_sem=rs,
            device_id={"ep": e, "etp": f}, device_id_type=MESH,
        )

    w_copies = [
        pltpu.make_async_copy(h.at[0], v, sem_w.at[i])
        for i, (h, v) in enumerate(((wg_h, wg), (wu_h, wu), (wd_h, wd)))
    ]
    in_copies = [
        pltpu.make_async_copy(h, v, sem_in.at[i])
        for i, (h, v) in enumerate(((tokens, tok_v), (gout, gout_v), (ids_h, ids), (probs_h, probs)))
    ]
    for i in (2, 3, 0, 1):
        in_copies[i].start()

    barrier = pltpu.get_barrier_semaphore()

    @pl.loop(1, SLOTS)
    def _(j):
        pl.semaphore_signal(barrier, inc=1, device_id={"ep": target(j), "etp": t}, device_id_type=MESH)

    for f in (t_up, t_down, t_far, t_sib):
        pl.semaphore_signal(barrier, inc=1, device_id={"ep": ep, "etp": f}, device_id_type=MESH)

    for copy in w_copies:
        copy.start()
    in_copies[2].wait()
    in_copies[3].wait()

    lane = lax.broadcasted_iota(jnp.int32, (128, 128), 1)
    row = lax.broadcasted_iota(jnp.int32, (128, 128), 0)
    j = lax.broadcasted_iota(jnp.int32, (SLOTS, 128), 0)
    ji = j & 3
    expert = ((z + ji) & 3) * 4 + ((x + ji + (j >> 2)) & 3)
    hit = jnp.zeros((SLOTS, 128), F32)
    weight = jnp.zeros((SLOTS, 128), F32)
    for k in range(ids.shape[0]):
        same = ids[k : k + 1, :] == expert
        hit = hit + jnp.where(same, 1.0, 0.0)
        weight = weight + jnp.where(same, probs[k : k + 1, :], 0.0)
    earlier = jnp.where(row < lane, 1.0, 0.0).astype(BF)
    pos = nn(hit.astype(BF), earlier)
    rank = lax.broadcasted_iota(jnp.int32, (CAP, 128), 0).astype(F32)
    for j in range(SLOTS):
        one = jnp.where(pos[j : j + 1] == rank, hit[j : j + 1], 0.0)
        place[j * CAP : (j + 1) * CAP, :] = one.astype(BF)
        pw[j * CAP : (j + 1) * CAP, :] = jnp.broadcast_to(
            jnp.sum(one * weight[j : j + 1], axis=1, keepdims=True), (CAP, 128)
        )

    raw_copies = [
        remote(src, raw.at[i], sem_raw.at[0, i], sem_raw.at[1, i], ep, t_far)
        for i, src in enumerate((tokens, gout))
    ]

    def fill(b, g, tok, grad):
        rows = pl.ds(g * 192, 192)
        one = place[rows, :]
        snd[b, 0, rows, :] = nn(one, tok).astype(BF)
        snd[b, 1, rows, :] = (nn(one, grad) * pw[rows, 0:1]).astype(BF)

    def own_copy(b):
        f = (t, t_far)[b]
        return pltpu.make_async_copy(
            snd.at[b, :, pl.ds(0, CAP), :], xg.at[:, pl.ds(0, CAP), cols(f)], sem_self.at[b]
        )

    def out_copy(b, j, e):
        f = (t, t_far)[b]
        return remote(
            snd.at[b, :, slot(j), :], xg.at[:, slot(j), cols(f)],
            sem_send.at[b], sem_recv.at[b, j // UNIT], e, t,
        )

    def send(b, u):
        for j in range(u * UNIT, (u + 1) * UNIT):
            if j == 0:
                own_copy(b).start()
            else:
                out_copy(b, j, target(j)).start()

    def fwd_copy(kind, u):
        rows = pl.ds(u * UROWS, UROWS)
        f = (t, t, t, t_far, t_down, t_up)[kind]
        to = (t_up, t_down, t_sib, t_sib, t_sib, t_sib)[kind]
        ref = xg.at[:, rows, cols(f)]
        if kind < 2:
            return remote(ref, ref, sem_fsend.at[0], sem_yget.at[kind, u], ep, to)
        return remote(ref, ref, sem_fsend.at[1], sem_sget.at[min(u // 3, 2)], ep, to)

    def got(b, u):
        first = max(1, u * UNIT)
        rows = pl.ds(first * CAP, ((u + 1) * UNIT - first) * CAP)
        if u == 0:
            own_copy(b).wait()
        ref = xg.at[:, rows, cols((t, t_far)[b])]
        remote(ref, ref, sem_send.at[b], sem_recv.at[b, u], ep, t_sib).wait_recv()

    def fwd_a(u):
        got(0, u)
        for kind in (0, 1, 2):
            fwd_copy(kind, u).start()

    def fwd_b(u):
        got(1, u)
        fwd_copy(3, u).start()

    def fwd_y(u):
        rows = pl.ds(u * UROWS, UROWS)
        for kind in (0, 1):
            ref = xg.at[:, rows, cols((t_down, t_up)[kind])]
            remote(ref, ref, sem_fsend.at[0], sem_yget.at[kind, u], ep, t_sib).wait_recv()
            fwd_copy(4 + kind, u).start()

    def whole(c):
        first, last = ((0, 3), (3, 6), (6, 8))[c]
        ref = xg.at[:, pl.ds(first * UROWS, (last - first) * UROWS), pl.ds(0, 4 * width)]
        remote(ref, ref, sem_fsend.at[1], sem_sget.at[c], ep, t_sib).wait_recv()

    in_copies[0].wait()
    in_copies[1].wait()
    fill(0, 0, tok_v[...], gout_v[...])
    pl.semaphore_wait(barrier, SLOTS - 1 + 4)
    for copy in raw_copies:
        copy.start()
    send(0, 0)
    send(0, 1)
    fill(0, 1, tok_v[...], gout_v[...])
    send(0, 2)
    send(0, 3)
    fill(0, 2, tok_v[...], gout_v[...])
    fill(0, 3, tok_v[...], gout_v[...])
    fwd_a(0)
    fwd_a(1)
    for copy in raw_copies:
        copy.wait_recv()
    fill(1, 0, raw[0], raw[1])
    send(1, 0)
    send(1, 1)
    fill(1, 1, raw[0], raw[1])
    send(1, 2)
    fwd_a(2)
    send(0, 4)
    send(0, 5)
    send(1, 3)
    fill(1, 2, raw[0], raw[1])
    send(1, 4)
    send(1, 5)
    fill(1, 3, raw[0], raw[1])
    send(0, 6)
    send(0, 7)
    send(1, 6)
    send(1, 7)

    def tiles(n, body, services=None):
        services = services or {}

        @pl.loop(0, n)
        def _(k):
            body(k)
            for at, calls in services.items():
                @pl.when(k == at)
                def _():
                    for call in calls:
                        call()

    def forward(c, services):
        rows = pl.ds(c * CHUNK, CHUNK)
        for acc, side, w, calls in ((acc_g, 0, wg, services[0]), (acc_u, 0, wu, services[1]), (acc_h, 1, wd, services[2])):
            acc[...] = nt(xg[side, rows, :], w[...])
            for call in calls:
                call()
        piece = 64

        @pl.loop(0, CHUNK // piece)
        def _(i):
            rs = pl.ds(pl.multiple_of(i * piece, piece), piece)
            rd = pl.ds(pl.multiple_of(c * CHUNK + i * piece, piece), piece)
            g = acc_g[rs, :]
            u = acc_u[rs, :]
            h = acc_h[rs, :]
            s = jax.nn.sigmoid(g)
            sg = g * s
            hid[rd, :] = (sg * u).astype(BF)
            gpg[rd, :] = (h * u * s * (1.0 + g * (1.0 - s))).astype(BF)
            gpu[rd, :] = (h * sg).astype(BF)

    steps = (1, 3, 2, 0)

    def chunk_rows(c):
        return pl.ds(c * CHUNK, CHUNK)

    def sib_copy(c, i):
        rows = chunk_rows(c)
        return remote(
            part.at[i, 1 - core, rows, :], from_sib.at[i, rows, :],
            sem_psend.at[0], sem_precv.at[c, i], ep, t_sib,
        )

    def y_copy(c, i):
        rows = chunk_rows(c)
        return remote(
            part.at[i, core, rows, :], from_y.at[i, rows, :],
            sem_ysend.at[0], sem_yrecv.at[c, i], ep, (t_up, t_down)[i],
        )

    def quarter(c, i):
        rows = chunk_rows(c)
        q = (y + steps[i]) % 4
        ws = pl.ds(pl.multiple_of(q * 2 * width, 128), 2 * width)
        p = nn(gpg[rows, :], wg[:, ws]) + nn(gpu[rows, :], wu[:, ws])
        part[i, 0, rows, :] = p[:, :width].astype(BF)
        part[i, 1, rows, :] = p[:, width:].astype(BF)
        sib_copy(c, i).start()

    def pair(c, i):
        rows = chunk_rows(c)
        sib_copy(c, i).wait_recv()
        return part[i, core, rows, :].astype(F32) + from_sib[i, rows, :].astype(F32)

    def pair_y(c, i):
        part[i, core, chunk_rows(c), :] = pair(c, i).astype(BF)
        y_copy(c, i).start()

    def back_copy(b, j, e):
        return remote(
            snd_back.at[b, slot(j), :], back.at[b, slot(j), :],
            sem_bsend.at[0], sem_brecv.at[b], e, t,
        )

    def own_back(b):
        return pltpu.make_async_copy(
            snd_back.at[b, pl.ds(0, CAP), :], back.at[b, pl.ds(0, CAP), :], sem_bself.at[b]
        )

    def send_back(c, b):
        for j in range(BACK[c], BACK[c + 1]):
            if j == 0:
                own_back(b).start()
            else:
                back_copy(b, j, source(j)).start()

    def pair_far(c):
        snd_back[1, chunk_rows(c), :] = pair(c, 2).astype(BF)
        send_back(c, 1)

    def pair_own(c):
        rows = chunk_rows(c)
        mine = pair(c, 3)
        for i in (0, 1):
            y_copy(c, i).wait_recv()
            mine = mine + from_y[i, rows, :].astype(F32)
        snd_back[0, rows, :] = mine.astype(BF)
        send_back(c, 0)

    tail = remote(tail_snd, tail_rcv, sem_tail.at[0], sem_tail.at[1], ep, t_far)

    others = pl.ds(CAP, ROWS - CAP)

    def got_back(b):
        own_back(b).wait()
        remote(
            snd_back.at[b, others, :], back.at[b, others, :], sem_bsend.at[0], sem_brecv.at[b], ep, t_sib
        ).wait_recv()

    def combine_far():
        got_back(1)
        tail_snd[...] = tn(place[...], back[1]).astype(BF)
        tail.start()

    def combine_own():
        got_back(0)
        mine = tn(place[...], back[0])
        tail.wait_recv()
        gt_out[...] = (mine + tail_rcv[...].astype(F32)).astype(BF)

    wt = 1024

    def grad_tile(i, k):
        ks = pl.ds(pl.multiple_of(k * wt, wt), wt)
        (gd_h, gg_h, gu_h)[i][0, :, ks] = tn((hid, gpg, gpu)[i][...], xg[(1, 0, 0)[i], :, ks]).astype(BF)

    nw = xg.shape[2] // wt

    def act(f, *args):
        return lambda: f(*args)

    def back_part(c, calls):
        quarter(c, 0)
        quarter(c, 1)
        pair_y(c, 0)
        for call in calls[0]:
            call()
        quarter(c, 2)
        pair_y(c, 1)
        for call in calls[1]:
            call()
        quarter(c, 3)
        pair_far(c)
        for call in calls[2]:
            call()

    fwd_a(3)
    fwd_y(0)
    fwd_b(0)
    fwd_b(1)
    fwd_y(1)
    fwd_b(2)
    fwd_a(4)
    fwd_y(2)
    for copy in w_copies:
        copy.wait()
    whole(0)
    forward(0, ([act(fwd_a, 5), act(fwd_y, 3)], [act(fwd_b, 3)], [act(fwd_b, 4), act(fwd_y, 4)]))
    back_part(0, ([act(fwd_a, 6), act(fwd_b, 5)], [act(fwd_a, 7)], []))
    fwd_y(5)
    whole(1)
    forward(1, ([], [act(fwd_b, 6)], [act(fwd_y, 6)]))
    back_part(1, ([act(fwd_b, 7)], [], []))
    fwd_y(7)
    whole(2)
    forward(2, ([act(pair_own, 0)], [], [act(pair_own, 1)]))
    back_part(2, ([], [], []))
    tiles(nw, lambda k: grad_tile(0, k), {1: [act(pair_own, 2)]})
    tiles(nw, lambda k: grad_tile(1, k), {0: [combine_far]})
    tiles(nw, lambda k: grad_tile(2, k), {1: [combine_own]})

    for copy in raw_copies:
        copy.wait_send()
    tail.wait_send()
    for b in (0, 1):
        remote(
            snd.at[b, :, others, :], xg.at[:, others, pl.ds(0, width)], sem_send.at[b], sem_recv.at[b, 0], ep, t_sib
        ).wait_send()
    ref = xg.at[:, :, pl.ds(0, 2 * width)]
    remote(ref, ref, sem_fsend.at[0], sem_sget.at[0], ep, t_sib).wait_send()
    ref = xg.at[:, :, pl.ds(0, 4 * width)]
    remote(ref, ref, sem_fsend.at[1], sem_sget.at[0], ep, t_sib).wait_send()
    remote(from_sib, from_sib, sem_psend.at[0], sem_precv.at[0, 0], ep, t_sib).wait_send()
    remote(from_y, from_y, sem_ysend.at[0], sem_yrecv.at[0, 0], ep, t_sib).wait_send()
    ref = snd_back.at[:, others, :]
    remote(ref, ref, sem_bsend.at[0], sem_brecv.at[0], ep, t_sib).wait_send()


def local(tokens, grad_out, probs, expert_ids, w_gate, w_up, w_down):
    toks, width = tokens.shape
    _, d, ff = w_gate.shape
    w_gate = w_gate.transpose(0, 2, 1)
    w_up = w_up.transpose(0, 2, 1)
    vmem = pl.BlockSpec(memory_space=pltpu.VMEM)
    hbm = pl.BlockSpec(memory_space=pl.ANY)
    dma = pltpu.SemaphoreType.DMA
    n = CHUNK
    gt, gg, gu, gd = pl.pallas_call(
        expert_kernel,
        out_shape=[
            jax.ShapeDtypeStruct((toks, width), BF),
            pltpu.VMEM(w_gate.shape, BF),
            pltpu.VMEM(w_up.shape, BF),
            pltpu.VMEM(w_down.shape, BF),
        ],
        in_specs=[hbm] * 7,
        out_specs=[vmem] * 4,
        scratch_shapes=[
            pltpu.VMEM((2, ROWS, d), BF),
            pltpu.VMEM((2, 2, ROWS, width), BF),
            pltpu.VMEM((2, toks, width), BF),
            pltpu.VMEM((toks, width), BF),
            pltpu.VMEM((toks, width), BF),
            pltpu.VMEM(expert_ids.T.shape, jnp.int32),
            pltpu.VMEM(probs.T.shape, F32),
            pltpu.VMEM((ff, d), BF),
            pltpu.VMEM((ff, d), BF),
            pltpu.VMEM((ff, d), BF),
            pltpu.VMEM((ROWS, toks), BF),
            pltpu.VMEM((ROWS, 128), F32),
            pltpu.VMEM((ROWS, ff), BF),
            pltpu.VMEM((ROWS, ff), BF),
            pltpu.VMEM((ROWS, ff), BF),
            pltpu.VMEM((n, ff), F32),
            pltpu.VMEM((n, ff), F32),
            pltpu.VMEM((n, ff), F32),
            pltpu.VMEM((4, 2, ROWS, width), BF),
            pltpu.VMEM((4, ROWS, width), BF),
            pltpu.VMEM((2, ROWS, width), BF),
            pltpu.VMEM((2, ROWS, width), BF),
            pltpu.VMEM((2, ROWS, width), BF),
            pltpu.VMEM((toks, width), BF),
            pltpu.VMEM((toks, width), BF),
            dma((4,)),
            dma((3,)),
            dma((2, 2)),
            dma((2,)),
            dma((2,)),
            dma((2, UNITS)),
            dma((2,)),
            dma((2, UNITS)),
            dma((CHUNKS,)),
            dma((1,)),
            dma((CHUNKS, 4)),
            dma((1,)),
            dma((CHUNKS, 2)),
            dma((2,)),
            dma((1,)),
            dma((2,)),
            dma((2,)),
        ],
        compiler_params=pltpu.CompilerParams(
            collective_id=0, has_side_effects=True, vmem_limit_bytes=46 * 2**20
        ),
    )(tokens, grad_out, expert_ids.T, probs.T, w_gate, w_up, w_down)
    return gt, gg.transpose(0, 2, 1), gu.transpose(0, 2, 1), gd


def solution(mesh):
    return jax.shard_map(
        local,
        mesh=mesh,
        in_specs=(
            P("ep", "etp"),
            P("ep", "etp"),
            P("ep", None),
            P("ep", None),
            P("ep", None, "etp"),
            P("ep", None, "etp"),
            P("ep", "etp", None),
        ),
        out_specs=(
            P("ep", "etp"),
            P("ep", None, "etp"),
            P("ep", None, "etp"),
            P("ep", "etp", None),
        ),
        check_vma=False,
    )
```

```python
import functools
import jax
import jax.numpy as jnp
from jax import lax
from jax.experimental import pallas as pl
from jax.experimental.pallas import tpu as pltpu
from jax.sharding import PartitionSpec as P

BF = jnp.bfloat16
F32 = jnp.float32
CAP = 48
SLOTS = 16
ROWS = CAP * SLOTS
UNIT = 2
UROWS = UNIT * CAP
UNITS = SLOTS // UNIT
EDGES = (0, 192, 480, ROWS)
CHUNKS = len(EDGES) - 1
BACK = (0, 4, 10, SLOTS)
MESH = pl.DeviceIdType.MESH


def nt(a, b):
    return lax.dot_general(a, b, (((1,), (1,)), ((), ())), preferred_element_type=F32)


def tn(a, b):
    return lax.dot_general(a, b, (((0,), (0,)), ((), ())), preferred_element_type=F32)


def nn(a, b):
    return jnp.dot(a, b, preferred_element_type=F32)


def expert_kernel(
    tokens, gout, ids_h, probs_h, wg_h, wu_h, wd_h,
    gt_out, gg_h, gu_h, gd_h,
    xg, snd, raw, tok_v, gout_v, ids, probs, wg, wu, wd, place, pw,
    hid, gpg, gpu, acc_g, acc_u, acc_h,
    part, from_sib, from_y, snd_back, back, tail_snd, tail_rcv,
    sem_in, sem_w, sem_raw, sem_self, sem_send, sem_recv, sem_fsend, sem_yget, sem_sget,
    sem_psend, sem_precv, sem_ysend, sem_yrecv, sem_bself, sem_bsend, sem_brecv, sem_tail,
):
    ep = lax.axis_index("ep")
    t = lax.axis_index("etp")
    z, x = ep // 4, ep % 4
    y, core = t // 2, t % 2
    width = tokens.shape[1]
    t_up, t_down, t_far = (t + 2) % 8, (t + 6) % 8, (t + 4) % 8
    t_sib = t + 1 - 2 * core

    def target(j):
        i = j % 4
        return ((z + i) % 4) * 4 + (x + i + j // 4) % 4

    def source(j):
        i = j % 4
        return ((z + 4 - i) % 4) * 4 + (x + 8 - i - j // 4) % 4

    def cols(f):
        return pl.ds(pl.multiple_of(f * width, 128), width)

    def slot(j):
        return pl.ds(pl.multiple_of(j * CAP, 16), CAP)

    def remote(src, dst, ss, rs, e, f):
        return pltpu.make_async_remote_copy(
            src_ref=src, dst_ref=dst, send_sem=ss, recv_sem=rs,
            device_id={"ep": e, "etp": f}, device_id_type=MESH,
        )

    w_copies = [
        pltpu.make_async_copy(h.at[0], v, sem_w.at[i])
        for i, (h, v) in enumerate(((wg_h, wg), (wu_h, wu), (wd_h, wd)))
    ]
    in_copies = [
        pltpu.make_async_copy(h, v, sem_in.at[i])
        for i, (h, v) in enumerate(((tokens, tok_v), (gout, gout_v), (ids_h, ids), (probs_h, probs)))
    ]
    for i in (2, 3, 0, 1):
        in_copies[i].start()

    barrier = pltpu.get_barrier_semaphore()

    @pl.loop(1, SLOTS)
    def _(j):
        pl.semaphore_signal(barrier, inc=1, device_id={"ep": target(j), "etp": t}, device_id_type=MESH)

    for f in (t_up, t_down, t_far, t_sib):
        pl.semaphore_signal(barrier, inc=1, device_id={"ep": ep, "etp": f}, device_id_type=MESH)

    for copy in w_copies:
        copy.start()
    in_copies[2].wait()
    in_copies[3].wait()

    lane = lax.broadcasted_iota(jnp.int32, (128, 128), 1)
    row = lax.broadcasted_iota(jnp.int32, (128, 128), 0)
    j = lax.broadcasted_iota(jnp.int32, (SLOTS, 128), 0)
    ji = j & 3
    expert = ((z + ji) & 3) * 4 + ((x + ji + (j >> 2)) & 3)
    hit = jnp.zeros((SLOTS, 128), F32)
    weight = jnp.zeros((SLOTS, 128), F32)
    for k in range(ids.shape[0]):
        same = ids[k : k + 1, :] == expert
        hit = hit + jnp.where(same, 1.0, 0.0)
        weight = weight + jnp.where(same, probs[k : k + 1, :], 0.0)
    earlier = jnp.where(row < lane, 1.0, 0.0).astype(BF)
    pos = nn(hit.astype(BF), earlier)
    rank = lax.broadcasted_iota(jnp.int32, (CAP, 128), 0).astype(F32)
    for j in range(SLOTS):
        one = jnp.where(pos[j : j + 1] == rank, hit[j : j + 1], 0.0)
        place[j * CAP : (j + 1) * CAP, :] = one.astype(BF)
        pw[j * CAP : (j + 1) * CAP, :] = jnp.broadcast_to(
            jnp.sum(one * weight[j : j + 1], axis=1, keepdims=True), (CAP, 128)
        )

    raw_copies = [
        remote(src, raw.at[i], sem_raw.at[0, i], sem_raw.at[1, i], ep, t_far)
        for i, src in enumerate((tokens, gout))
    ]

    def fill(b, g, tok, grad):
        rows = pl.ds(g * 192, 192)
        one = place[rows, :]
        snd[b, 0, rows, :] = nn(one, tok).astype(BF)
        snd[b, 1, rows, :] = (nn(one, grad) * pw[rows, 0:1]).astype(BF)

    def own_copy(b):
        f = (t, t_far)[b]
        return pltpu.make_async_copy(
            snd.at[b, :, pl.ds(0, CAP), :], xg.at[:, pl.ds(0, CAP), cols(f)], sem_self.at[b]
        )

    def out_copy(b, j, e):
        f = (t, t_far)[b]
        return remote(
            snd.at[b, :, slot(j), :], xg.at[:, slot(j), cols(f)],
            sem_send.at[b], sem_recv.at[b, j // UNIT], e, t,
        )

    def send(b, u):
        for j in range(u * UNIT, (u + 1) * UNIT):
            if j == 0:
                own_copy(b).start()
            else:
                out_copy(b, j, target(j)).start()

    def fwd_copy(kind, u):
        rows = pl.ds(u * UROWS, UROWS)
        f = (t, t, t, t_far, t_down, t_up)[kind]
        to = (t_up, t_down, t_sib, t_sib, t_sib, t_sib)[kind]
        ref = xg.at[:, rows, cols(f)]
        if kind < 2:
            return remote(ref, ref, sem_fsend.at[0], sem_yget.at[kind, u], ep, to)
        return remote(ref, ref, sem_fsend.at[1], sem_sget.at[(u + 1) // 3], ep, to)

    def got(b, u):
        first = max(1, u * UNIT)
        rows = pl.ds(first * CAP, ((u + 1) * UNIT - first) * CAP)
        if u == 0:
            own_copy(b).wait()
        ref = xg.at[:, rows, cols((t, t_far)[b])]
        remote(ref, ref, sem_send.at[b], sem_recv.at[b, u], ep, t_sib).wait_recv()

    def fwd_a(u):
        got(0, u)
        for kind in (0, 1, 2):
            fwd_copy(kind, u).start()

    def fwd_b(u):
        got(1, u)
        fwd_copy(3, u).start()

    def fwd_y(u):
        rows = pl.ds(u * UROWS, UROWS)
        for kind in (0, 1):
            ref = xg.at[:, rows, cols((t_down, t_up)[kind])]
            remote(ref, ref, sem_fsend.at[0], sem_yget.at[kind, u], ep, t_sib).wait_recv()
            fwd_copy(4 + kind, u).start()

    def whole(c):
        ref = xg.at[:, pl.ds(EDGES[c], EDGES[c + 1] - EDGES[c]), pl.ds(0, 4 * width)]
        remote(ref, ref, sem_fsend.at[1], sem_sget.at[c], ep, t_sib).wait_recv()

    in_copies[0].wait()
    in_copies[1].wait()
    fill(0, 0, tok_v[...], gout_v[...])
    pl.semaphore_wait(barrier, SLOTS - 1 + 4)
    for copy in raw_copies:
        copy.start()
    send(0, 0)
    send(0, 1)
    fill(0, 1, tok_v[...], gout_v[...])
    send(0, 2)
    send(0, 3)
    fill(0, 2, tok_v[...], gout_v[...])
    fill(0, 3, tok_v[...], gout_v[...])
    fwd_a(0)
    fwd_a(1)
    for copy in raw_copies:
        copy.wait_recv()
    fill(1, 0, raw[0], raw[1])
    send(1, 0)
    send(1, 1)
    send(0, 4)
    fwd_a(2)
    fill(1, 1, raw[0], raw[1])
    send(1, 2)
    send(0, 5)
    send(1, 3)
    send(0, 6)
    fill(1, 2, raw[0], raw[1])
    send(1, 4)
    send(0, 7)
    send(1, 5)
    fill(1, 3, raw[0], raw[1])
    send(1, 6)
    send(1, 7)

    def tiles(n, body, services=None):
        services = services or {}

        @pl.loop(0, n)
        def _(k):
            body(k)
            for at, calls in services.items():
                @pl.when(k == at)
                def _():
                    for call in calls:
                        call()

    def forward(c, services):
        rows = pl.ds(EDGES[c], EDGES[c + 1] - EDGES[c])
        for acc, side, w, calls in ((acc_g, 0, wg, services[0]), (acc_u, 0, wu, services[1]), (acc_h, 1, wd, services[2])):
            acc[0 : EDGES[c + 1] - EDGES[c], :] = nt(xg[side, rows, :], w[...])
            for call in calls:
                call()
        piece = 96

        @pl.loop(0, (EDGES[c + 1] - EDGES[c]) // piece)
        def _(i):
            rs = pl.ds(pl.multiple_of(i * piece, piece), piece)
            rd = pl.ds(pl.multiple_of(EDGES[c] + i * piece, piece), piece)
            g = acc_g[rs, :]
            u = acc_u[rs, :]
            h = acc_h[rs, :]
            s = jax.nn.sigmoid(g)
            sg = g * s
            hid[rd, :] = (sg * u).astype(BF)
            gpg[rd, :] = (h * u * s * (1.0 + g * (1.0 - s))).astype(BF)
            gpu[rd, :] = (h * sg).astype(BF)

    steps = (1, 3, 2, 0)

    def chunk_rows(c):
        return pl.ds(EDGES[c], EDGES[c + 1] - EDGES[c])

    def sib_copy(c, i):
        rows = chunk_rows(c)
        return remote(
            part.at[i, 1 - core, rows, :], from_sib.at[i, rows, :],
            sem_psend.at[0], sem_precv.at[c, i], ep, t_sib,
        )

    def y_copy(c, i):
        rows = chunk_rows(c)
        return remote(
            part.at[i, core, rows, :], from_y.at[i, rows, :],
            sem_ysend.at[0], sem_yrecv.at[c, i], ep, (t_up, t_down)[i],
        )

    def quarter(c, i):
        rows = chunk_rows(c)
        q = (y + steps[i]) % 4
        ws = pl.ds(pl.multiple_of(q * 2 * width, 128), 2 * width)
        p = nn(gpg[rows, :], wg[:, ws]) + nn(gpu[rows, :], wu[:, ws])
        part[i, 0, rows, :] = p[:, :width].astype(BF)
        part[i, 1, rows, :] = p[:, width:].astype(BF)
        sib_copy(c, i).start()

    def pair(c, i):
        rows = chunk_rows(c)
        sib_copy(c, i).wait_recv()
        return part[i, core, rows, :].astype(F32) + from_sib[i, rows, :].astype(F32)

    def pair_y(c, i):
        part[i, core, chunk_rows(c), :] = pair(c, i).astype(BF)
        y_copy(c, i).start()

    def back_copy(b, j, e):
        return remote(
            snd_back.at[b, slot(j), :], back.at[b, slot(j), :],
            sem_bsend.at[0], sem_brecv.at[b], e, t,
        )

    def own_back(b):
        return pltpu.make_async_copy(
            snd_back.at[b, pl.ds(0, CAP), :], back.at[b, pl.ds(0, CAP), :], sem_bself.at[b]
        )

    def send_back(c, b):
        for j in range(BACK[c], BACK[c + 1]):
            if j == 0:
                own_back(b).start()
            else:
                back_copy(b, j, source(j)).start()

    def pair_far(c):
        snd_back[1, chunk_rows(c), :] = pair(c, 2).astype(BF)
        send_back(c, 1)

    def pair_own(c):
        rows = chunk_rows(c)
        mine = pair(c, 3)
        for i in (0, 1):
            y_copy(c, i).wait_recv()
            mine = mine + from_y[i, rows, :].astype(F32)
        snd_back[0, rows, :] = mine.astype(BF)
        send_back(c, 0)

    tail = remote(tail_snd, tail_rcv, sem_tail.at[0], sem_tail.at[1], ep, t_far)

    others = pl.ds(CAP, ROWS - CAP)

    def got_back(b):
        own_back(b).wait()
        remote(
            snd_back.at[b, others, :], back.at[b, others, :], sem_bsend.at[0], sem_brecv.at[b], ep, t_sib
        ).wait_recv()

    def combine_far():
        got_back(1)
        tail_snd[...] = tn(place[...], back[1]).astype(BF)
        tail.start()

    def combine_own():
        got_back(0)
        mine = tn(place[...], back[0])
        tail.wait_recv()
        gt_out[...] = (mine + tail_rcv[...].astype(F32)).astype(BF)

    wt = 1024

    def grad_tile(i, k):
        ks = pl.ds(pl.multiple_of(k * wt, wt), wt)
        (gd_h, gg_h, gu_h)[i][0, :, ks] = tn((hid, gpg, gpu)[i][...], xg[(1, 0, 0)[i], :, ks]).astype(BF)

    nw = xg.shape[2] // wt

    def act(f, *args):
        return lambda: f(*args)

    def back_part(c, calls, hold=False):
        quarter(c, 0)
        quarter(c, 1)
        if not hold:
            pair_y(c, 0)
        for call in calls[0]:
            call()
        quarter(c, 2)
        if not hold:
            pair_y(c, 1)
        for call in calls[1]:
            call()
        quarter(c, 3)
        pair_far(c)
        for call in calls[2]:
            call()

    fwd_a(3)
    fwd_y(0)
    fwd_b(0)
    fwd_b(1)
    fwd_y(1)
    for copy in w_copies:
        copy.wait()
    whole(0)
    forward(0, ([act(fwd_a, 4)], [act(fwd_y, 2), act(fwd_b, 2)], [act(fwd_a, 5)]))
    back_part(0, ([act(fwd_b, 3), act(fwd_y, 3)], [act(fwd_a, 6)], []), hold=True)
    fwd_b(4)
    fwd_y(4)
    whole(1)
    forward(1, ([act(fwd_a, 7)], [act(fwd_b, 5), act(fwd_y, 5)], [act(pair_y, 0, 0), act(pair_y, 0, 1)]))
    back_part(1, ([act(fwd_b, 6), act(fwd_y, 6)], [], [act(fwd_b, 7)]))
    fwd_y(7)
    whole(2)
    forward(2, ([], [], [act(pair_own, 0)]))
    back_part(2, ([], [], [act(pair_own, 1)]))
    tiles(nw, lambda k: grad_tile(0, k), {1: [act(pair_own, 2)]})
    tiles(nw, lambda k: grad_tile(1, k), {0: [combine_far]})
    tiles(nw, lambda k: grad_tile(2, k), {1: [combine_own]})

    for copy in raw_copies:
        copy.wait_send()
    tail.wait_send()
    for b in (0, 1):
        remote(
            snd.at[b, :, others, :], xg.at[:, others, pl.ds(0, width)], sem_send.at[b], sem_recv.at[b, 0], ep, t_sib
        ).wait_send()
    ref = xg.at[:, :, pl.ds(0, 2 * width)]
    remote(ref, ref, sem_fsend.at[0], sem_sget.at[0], ep, t_sib).wait_send()
    ref = xg.at[:, :, pl.ds(0, 4 * width)]
    remote(ref, ref, sem_fsend.at[1], sem_sget.at[0], ep, t_sib).wait_send()
    remote(from_sib, from_sib, sem_psend.at[0], sem_precv.at[0, 0], ep, t_sib).wait_send()
    remote(from_y, from_y, sem_ysend.at[0], sem_yrecv.at[0, 0], ep, t_sib).wait_send()
    ref = snd_back.at[:, others, :]
    remote(ref, ref, sem_bsend.at[0], sem_brecv.at[0], ep, t_sib).wait_send()


def leave_kernel(*refs):
    n = len(refs) // 2
    copies = [pltpu.make_async_copy(refs[i], refs[n + i], refs[-1].at[i]) for i in range(n)]
    for copy in copies:
        copy.start()
    for copy in copies:
        copy.wait()


def local(tokens, grad_out, probs, expert_ids, w_gate, w_up, w_down):
    toks, width = tokens.shape
    _, d, ff = w_gate.shape
    w_gate = w_gate.transpose(0, 2, 1)
    w_up = w_up.transpose(0, 2, 1)
    vmem = pl.BlockSpec(memory_space=pltpu.VMEM)
    hbm = pl.BlockSpec(memory_space=pl.ANY)
    dma = pltpu.SemaphoreType.DMA
    n = max(b - a for a, b in zip(EDGES, EDGES[1:]))
    results = pl.pallas_call(
        expert_kernel,
        out_shape=[
            pltpu.VMEM((toks, width), BF),
            pltpu.VMEM(w_gate.shape, BF),
            pltpu.VMEM(w_up.shape, BF),
            pltpu.VMEM(w_down.shape, BF),
        ],
        in_specs=[hbm] * 7,
        out_specs=[vmem] * 4,
        scratch_shapes=[
            pltpu.VMEM((2, ROWS, d), BF),
            pltpu.VMEM((2, 2, ROWS, width), BF),
            pltpu.VMEM((2, toks, width), BF),
            pltpu.VMEM((toks, width), BF),
            pltpu.VMEM((toks, width), BF),
            pltpu.VMEM(expert_ids.T.shape, jnp.int32),
            pltpu.VMEM(probs.T.shape, F32),
            pltpu.VMEM((ff, d), BF),
            pltpu.VMEM((ff, d), BF),
            pltpu.VMEM((ff, d), BF),
            pltpu.VMEM((ROWS, toks), BF),
            pltpu.VMEM((ROWS, 128), F32),
            pltpu.VMEM((ROWS, ff), BF),
            pltpu.VMEM((ROWS, ff), BF),
            pltpu.VMEM((ROWS, ff), BF),
            pltpu.VMEM((n, ff), F32),
            pltpu.VMEM((n, ff), F32),
            pltpu.VMEM((n, ff), F32),
            pltpu.VMEM((4, 2, ROWS, width), BF),
            pltpu.VMEM((4, ROWS, width), BF),
            pltpu.VMEM((2, ROWS, width), BF),
            pltpu.VMEM((2, ROWS, width), BF),
            pltpu.VMEM((2, ROWS, width), BF),
            pltpu.VMEM((toks, width), BF),
            pltpu.VMEM((toks, width), BF),
            dma((4,)),
            dma((3,)),
            dma((2, 2)),
            dma((2,)),
            dma((2,)),
            dma((2, UNITS)),
            dma((2,)),
            dma((2, UNITS)),
            dma((CHUNKS,)),
            dma((1,)),
            dma((CHUNKS, 4)),
            dma((1,)),
            dma((CHUNKS, 2)),
            dma((2,)),
            dma((1,)),
            dma((2,)),
            dma((2,)),
        ],
        compiler_params=pltpu.CompilerParams(
            collective_id=0, has_side_effects=True, vmem_limit_bytes=46 * 2**20
        ),
    )(tokens, grad_out, expert_ids.T, probs.T, w_gate, w_up, w_down)
    gt, gg, gu, gd = pl.pallas_call(
        leave_kernel,
        out_shape=[jax.ShapeDtypeStruct(r.shape, r.dtype) for r in results],
        in_specs=[hbm] * 4,
        out_specs=[hbm] * 4,
        scratch_shapes=[dma((4,))],
        compiler_params=pltpu.CompilerParams(vmem_limit_bytes=2**20),
    )(*results)
    return gt, gg.transpose(0, 2, 1), gu.transpose(0, 2, 1), gd


def solution(mesh):
    return jax.shard_map(
        local,
        mesh=mesh,
        in_specs=(
            P("ep", "etp"),
            P("ep", "etp"),
            P("ep", None),
            P("ep", None),
            P("ep", None, "etp"),
            P("ep", None, "etp"),
            P("ep", "etp", None),
        ),
        out_specs=(
            P("ep", "etp"),
            P("ep", None, "etp"),
            P("ep", None, "etp"),
            P("ep", "etp", None),
        ),
        check_vma=False,
    )
```
